128 devices in a mesh: loop: 8 (over z, core), grp: 16 (over y, x).
Axes of the slice: x: 4, y: 4, z: 4, core: 2. Of those that a mesh axis runs over, the one named last changes fastest.
Arguments:
- tokens: float32 [262144, 128], P(('loop', 'grp')), may hold values from -6 to 6
- filter_spec: float32 [2, 2048, 128, 2, 128], P(None, None, ('loop', 'grp')), may hold values from -5 to 5
- skip_gain: float32 [128], replicated, may hold values from 0.5 to 1.5
Outputs:
- mixed: float32 [262144, 128], P(('loop', 'grp'))
The draws below stay inside these ranges and needn't reach their ends.
All inputs are finite; a program needn't handle non-finite values.
Results may differ from the reference program's by a relative error of at most 0.000057.
Values sent between devices are 32-bit elements; how exact they have to be, the bound alone decides.
A program may use at most 128 MiB of HBM per device.

```python
import jax
import jax.numpy as jnp
from jax import lax

CHANNELS = 128
TOK_DEV = 2048
LENGTH = 262144
N_LOOP = 8
N_GRP = 16


def levels(rng, extent, shards, least, high):
    level, own = 1.0, jax.random.fold_in(rng, 6)
    for axis_at, blocks in shards:
        heights = jnp.exp(jax.random.uniform(jax.random.fold_in(own, axis_at), (blocks,), jnp.float32, least / len(shards), high / len(shards)))
        level = level * jnp.repeat(heights, extent[axis_at] // blocks).reshape([-1 if axis == axis_at else 1 for axis in range(len(extent))])
    return level


def gaussian(rng, dims, spread, bound, shards=(), held_as=jnp.bfloat16):
    result = jax.random.normal(rng, dims, jnp.float32) * spread
    if len(shards) > 0:
        result = levels(rng, dims, shards, -0.22, 0.18) * result
    return jnp.clip(result, min=-bound, max=bound).astype(held_as)


def setup_inputs(seed: int = 0) -> dict:
    arg_keys = jax.random.split(jax.random.key(seed), 4)
    tokens = gaussian(arg_keys[0], (LENGTH, CHANNELS), 1.0, 6.0, ((0, 128),), jnp.float32)
    filter_spec = gaussian(arg_keys[1], (2, TOK_DEV, N_LOOP * N_GRP, 2, CHANNELS), 1.0, 5.0, ((2, 128),), jnp.float32)
    skip_gain = jnp.clip(jax.random.uniform(arg_keys[2], (CHANNELS,), jnp.float32, 0.5, 1.5), 0.5, 1.5)
    return dict(tokens=tokens, filter_spec=filter_spec, skip_gain=skip_gain)


def reference(tokens, filter_spec, skip_gain):
    tok_total = tokens.shape[0]
    channels = tokens.shape[1]
    group_width = 16
    groups = channels // group_width
    token_groups = tokens.reshape(tok_total, groups, group_width).transpose(1, 0, 2)
    real_groups = filter_spec[0].reshape(2 * tok_total, groups, group_width).transpose(1, 0, 2)
    imag_groups = filter_spec[1].reshape(2 * tok_total, groups, group_width).transpose(1, 0, 2)

    def one_group(pieces):
        block_tokens, block_real, block_imag = pieces
        spectrum = jnp.fft.fft(block_tokens, n=2 * tok_total, axis=0)
        response = block_real + 1j * block_imag
        inverse = jnp.fft.ifft(spectrum * response, axis=0)
        return jnp.real(inverse[:tok_total]).astype(jnp.float32)

    convolved = lax.map(one_group, (token_groups, real_groups, imag_groups))
    convolved = convolved.transpose(1, 0, 2).reshape(tok_total, channels)
    return convolved + skip_gain[None, :] * tokens
```

```python
import functools
import math

import jax
import jax.numpy as jnp
from jax import lax
from jax.experimental import pallas as pl
from jax.experimental.pallas import tpu as pltpu
from jax.sharding import PartitionSpec as P

MESH = pl.DeviceIdType.MESH
PREC = lax.Precision.HIGH
DEV = 128


def peer(loop, grp, i):
    k = (i * 37) % DEV
    z = (loop // 2 + k // 16) % 4
    c = (loop + k // 64) % 2
    y = (grp // 4 + k // 4) % 4
    x = (grp + k) % 4
    return z * 2 + c, y * 4 + x


def swap_kernel(x_ref, o_ref, ssem, rsem, lsem):
    loop = lax.axis_index("loop")
    grp = lax.axis_index("grp")
    me = loop * 16 + grp
    bar = pltpu.get_barrier_semaphore()
    own = pltpu.make_async_copy(x_ref.at[me], o_ref.at[me], lsem)
    own.start()

    def greet(i, _):
        pl.semaphore_signal(bar, inc=1, device_id=peer(loop, grp, i), device_id_type=MESH)
        return 0

    lax.fori_loop(1, DEV, greet, 0)
    pl.semaphore_wait(bar, DEV - 1)

    def send(i, _):
        l, g = peer(loop, grp, i)
        pltpu.make_async_remote_copy(
            x_ref.at[l * 16 + g], o_ref.at[me], ssem, rsem, device_id=(l, g), device_id_type=MESH
        ).start()
        return 0

    lax.fori_loop(1, DEV, send, 0)
    whole = pltpu.make_async_remote_copy(
        x_ref.at[pl.ds(0, DEV - 1)],
        o_ref.at[pl.ds(0, DEV - 1)],
        ssem,
        rsem,
        device_id=(loop, grp),
        device_id_type=MESH,
    )
    whole.wait_send()
    whole.wait_recv()
    own.wait()


def swap(x, cid):
    return pl.pallas_call(
        swap_kernel,
        out_shape=jax.ShapeDtypeStruct(x.shape, x.dtype),
        in_specs=[pl.BlockSpec(memory_space=pl.ANY)],
        out_specs=pl.BlockSpec(memory_space=pl.ANY),
        scratch_shapes=[pltpu.SemaphoreType.DMA] * 3,
        compiler_params=pltpu.CompilerParams(collective_id=cid, has_side_effects=True),
    )(x)


def roots(numerator, denominator, direction):
    angles = (numerator % denominator).astype(jnp.float32) * (direction * 2.0 * math.pi / denominator)
    return jnp.cos(angles), jnp.sin(angles)


def body(tokens, filter_spec, skip_gain):
    me = lax.axis_index("loop") * 16 + lax.axis_index("grp")
    ein = functools.partial(jnp.einsum, precision=PREC)
    first = swap(tokens.reshape(DEV, 16, 128), 0)
    f = jnp.arange(256, dtype=jnp.int32)
    d = jnp.arange(DEV, dtype=jnp.int32)
    wc, ws = roots(f[:, None] * d[None, :], 256, -1.0)
    rows = me * 16 + jnp.arange(16, dtype=jnp.int32)
    tc, ts = roots(f[:, None] * rows[None, :], 524288, -1.0)
    tc, ts = tc[:, :, None], ts[:, :, None]
    re = ein("fn,nrx->frx", wc, first)
    im = ein("fn,nrx->frx", ws, first)
    twisted = jnp.stack([re * tc - im * ts, re * ts + im * tc], 1)
    second = swap(twisted.reshape(DEV, 64, 128), 1).reshape(DEV, 2, 2, 16, 128)
    gr, gi = second[:, :, 0], second[:, :, 1]
    kc, ks = roots(d[:, None] * d[None, :], 128, -1.0)
    ar = ein("ks,serx->kerx", kc, gr) - ein("ks,serx->kerx", ks, gi)
    ai = ein("ks,serx->kerx", kc, gi) + ein("ks,serx->kerx", ks, gr)
    r16 = jnp.arange(16, dtype=jnp.int32)
    bc, bs = roots(d[:, None] * r16[None, :], 2048, -1.0)
    bc, bs = bc[:, None, :, None], bs[:, None, :, None]
    ar, ai = ar * bc - ai * bs, ar * bs + ai * bc
    qc, qs = roots(r16[:, None] * r16[None, :], 16, -1.0)
    xr = ein("qr,kerx->qkex", qc, ar) - ein("qr,kerx->qkex", qs, ai)
    xi = ein("qr,kerx->qkex", qc, ai) + ein("qr,kerx->qkex", qs, ar)
    h = filter_spec.reshape(2, 16, DEV, 2, 128)
    pr, pi = xr * h[0] - xi * h[1], xr * h[1] + xi * h[0]
    ar = ein("qr,qkex->kerx", qc, pr) + ein("qr,qkex->kerx", qs, pi)
    ai = ein("qr,qkex->kerx", qc, pi) - ein("qr,qkex->kerx", qs, pr)
    ar, ai = ar * bc + ai * bs, ai * bc - ar * bs
    gr = ein("ks,kerx->serx", kc, ar) + ein("ks,kerx->serx", ks, ai)
    gi = ein("ks,kerx->serx", kc, ai) - ein("ks,kerx->serx", ks, ar)
    third = swap(jnp.stack([gr, gi], 2).reshape(DEV, 64, 128), 2).reshape(256, 2, 16, 128)
    re, im = third[:, 0], third[:, 1]
    re, im = re * tc + im * ts, im * tc - re * ts
    out = ein("fn,frx->nrx", wc, re) + ein("fn,frx->nrx", ws, im)
    fourth = swap(out, 3).reshape(2048, 128)
    return fourth * (1.0 / 524288.0) + skip_gain[None, :] * tokens


def solution(mesh):
    in_specs = (P(("loop", "grp"), None), P(None, None, ("loop", "grp"), None, None), P())
    out_specs = P(("loop", "grp"), None)
    return jax.shard_map(body, mesh=mesh, in_specs=in_specs, out_specs=out_specs, check_vma=False)
```

```python
import math

import jax
import jax.numpy as jnp
import numpy as np
from jax import lax
from jax.experimental import pallas as pl
from jax.experimental.pallas import tpu as pltpu
from jax.sharding import PartitionSpec as P

MESH = pl.DeviceIdType.MESH
DEV = 128
ROWS = 16
LANES = 128
FULL = 524288
STRIDE = 37


def split(value):
    high = value.astype(jnp.bfloat16)
    return high, (value - high.astype(jnp.float32)).astype(jnp.bfloat16)


def dot(a, b):
    return jnp.dot(a, b, preferred_element_type=jnp.float32)


def dot_three(a_high, a_low, b):
    b_high, b_low = split(b)
    return dot(a_high, b_high) + dot(a_high, b_low) + dot(a_low, b_high)


def roots(numerator, denominator):
    angles = -2.0 * math.pi * (np.asarray(numerator, np.int64) % denominator) / denominator
    return np.stack([np.cos(angles), np.sin(angles)])


def tables():
    row = np.arange(256)
    freq = 2 * (row % DEV) + row // DEV
    block = np.arange(DEV)
    base = roots(freq[:, None] * block[None, :], 256)
    shift = roots(freq[:, None] * block[None, :] * ROWS, FULL)
    step = np.broadcast_to(roots(freq, FULL)[:, :, None], (2, 256, LANES))
    columns = np.concatenate([base, shift, step]).reshape(6 * 256, LANES).astype(np.float32)
    base_t, shift_t = base.transpose(0, 2, 1) / FULL, shift.transpose(0, 2, 1)
    step_t = np.broadcast_to(roots(freq, FULL)[:, None, :], (2, 8, 256))
    across = np.concatenate([t.reshape(-1, 256) for t in (base_t, shift_t, step_t)]).astype(np.float32)
    cos, sin = roots(block[:, None] * block[None, :], DEV)
    forward = np.block([[cos, -sin], [sin, cos]]).astype(np.float32)
    both = np.concatenate([forward, forward.T])
    both_high = both.astype(jnp.bfloat16)
    both_low = (both - both_high.astype(np.float32)).astype(jnp.bfloat16)
    inner = np.concatenate([both_high, both_low])
    turn = roots(np.arange(ROWS)[:, None] * block[None, :], 2048).reshape(2 * ROWS * DEV, 1)
    turn = np.broadcast_to(turn, (2 * ROWS * DEV, LANES)).astype(np.float32)
    return columns, across, inner, turn


def peer(loop, grp, i):
    k = (i * STRIDE) % DEV
    z = (loop // 2 + k // 16) % 4
    c = (loop + k // 64) % 2
    y = (grp // 4 + k // 4) % 4
    x = (grp + k) % 4
    return z * 2 + c, y * 4 + x


def times(a, b):
    return a[0] * b[0] - a[1] * b[1], a[0] * b[1] + a[1] * b[0]


def times_conj(a, b):
    return a[0] * b[0] + a[1] * b[1], a[1] * b[0] - a[0] * b[1]


def four(a, b, c, d, forward):
    s0, s1 = (a[0] + c[0], a[1] + c[1]), (a[0] - c[0], a[1] - c[1])
    s2, s3 = (b[0] + d[0], b[1] + d[1]), (b[0] - d[0], b[1] - d[1])
    s3 = (s3[1], -s3[0]) if forward else (-s3[1], s3[0])
    return (
        (s0[0] + s2[0], s0[1] + s2[1]),
        (s1[0] + s3[0], s1[1] + s3[1]),
        (s0[0] - s2[0], s0[1] - s2[1]),
        (s1[0] - s3[0], s1[1] - s3[1]),
    )


def sixteen(values, forward):
    sign = -1.0 if forward else 1.0
    parts = []
    for low in range(4):
        out = four(*[values[4 * high + low] for high in range(4)], forward)
        turned = []
        for k, v in enumerate(out):
            m = low * k
            if m == 0:
                turned.append(v)
            elif m == 4:
                turned.append((-sign * v[1], sign * v[0]))
            else:
                angle = sign * 2.0 * math.pi * m / 16
                turned.append(times(v, (math.cos(angle), math.sin(angle))))
        parts.append(turned)
    result = [None] * 16
    for k in range(4):
        out = four(*[parts[low][k] for low in range(4)], forward)
        for high in range(4):
            result[k + 4 * high] = out[high]
    return result


def kernel(
    tokens, taps_hbm, gain, columns_hbm, across_hbm, inner_hbm, turn_hbm, mixed,
    first, send_two, second, middle, send_three, third, send_four,
    out_high, out_low, back_high, back_low, taps, columns, across, inner, turn,
    send_sem, recv_sem, local_sem,
):
    loop = lax.axis_index("loop")
    grp = lax.axis_index("grp")
    me = loop * 16 + grp
    bar = pltpu.get_barrier_semaphore()

    def rows(start, size):
        return pl.ds(pl.multiple_of(start, 8), size)

    loads = [
        pltpu.make_async_copy(src, dst, local_sem.at[n])
        for n, (src, dst) in enumerate(
            ((columns_hbm, columns), (across_hbm, across), (inner_hbm, inner), (turn_hbm, turn), (taps_hbm, taps))
        )
    ]
    for load in loads:
        load.start()

    def greet(i, _):
        pl.semaphore_signal(bar, inc=1, device_id=peer(loop, grp, i), device_id_type=MESH)
        return 0

    lax.fori_loop(1, DEV, greet, 0)
    pl.semaphore_wait(bar, DEV - 1)

    def scatter(src, dst, src_base, dst_base, size, n):
        own = pltpu.make_async_copy(
            src.at[rows(src_base + me * size, size)], dst.at[rows(dst_base + me * size, size)], local_sem.at[8 + n]
        )
        own.start()

        def send(i, _):
            l, g = peer(loop, grp, i)
            pltpu.make_async_remote_copy(
                src.at[rows(src_base + (l * 16 + g) * size, size)],
                dst.at[rows(dst_base + me * size, size)],
                send_sem.at[n],
                recv_sem.at[n],
                device_id=(l, g),
                device_id_type=MESH,
            ).start()
            return 0

        lax.fori_loop(1, DEV, send, 0)
        count = (DEV - 1) * size
        whole = pltpu.make_async_remote_copy(
            src.at[rows(src_base, count)],
            dst.at[rows(dst_base, count)],
            send_sem.at[n],
            recv_sem.at[n],
            device_id=(loop, grp),
            device_id_type=MESH,
        )
        return whole, own

    def arrive(move):
        move[0].wait_recv()
        move[1].wait()

    move_one = scatter(tokens, first, 0, 0, ROWS, 0)

    loads[0].wait()
    loads[1].wait()
    lane = lax.broadcasted_iota(jnp.int32, (16, LANES), 1)

    def build_out(t, _):
        at = pl.multiple_of(t * 16, 16)
        e, p = t // 8, pl.multiple_of((t % 8) * 16, 16)
        part = [columns[pl.ds(n * 256 + at, 16), :] for n in range(6)]
        shift = [jnp.sum(jnp.where(lane == me, v, 0.0), axis=1, keepdims=True) for v in part[2:4]]
        value = times(part[0:2], shift)
        for r in range(ROWS):
            for c in range(2):
                high, low = split(value[c])
                dst = pl.ds(((r * 2 + e) * 2 + c) * DEV + p, 16)
                out_high[dst, :] = high
                out_low[dst, :] = low
            if r < ROWS - 1:
                value = times(value, part[4:6])
        return 0

    lax.fori_loop(0, 16, build_out, 0)

    def build_back(t, _):
        at = pl.multiple_of(t * 16, 16)
        base = [across[pl.ds(n * DEV + at, 16), :] for n in range(2)]
        shift = [across[pl.ds((2 + n) * DEV + me, 1), :] for n in range(2)]
        step = [across[pl.ds(4 * DEV + n * 8, 1), :] for n in range(2)]
        value = times(base, shift)
        for r in range(ROWS):
            for c in range(2):
                high, low = split(value[c])
                dst = pl.ds((r * 2 + c) * DEV + at, 16)
                back_high[dst, :] = high
                back_low[dst, :] = low
            if r < ROWS - 1:
                value = times(value, step)
        return 0

    lax.fori_loop(0, 8, build_back, 0)

    arrive(move_one)
    move_two = []
    for e in range(2):
        for r in range(ROWS):
            at = (r * 2 + e) * 256
            value = dot_three(
                out_high[at : at + 256, :], out_low[at : at + 256, :], first[pl.ds(r, DEV, stride=ROWS), :]
            )
            for c in range(2):
                send_two[pl.ds(e * 4096 + c * ROWS + r, DEV, stride=2 * ROWS), :] = value[c * DEV : (c + 1) * DEV]
        move_two.append(scatter(send_two, second, e * 4096, e * 4096, 2 * ROWS, 1 + e))

    for load in loads[2:]:
        load.wait()

    move_three = []
    for e in range(2):
        arrive(move_two[e])
        for b in range(0, ROWS, 2):
            value = jnp.concatenate(
                [
                    jnp.concatenate(
                        [second[pl.ds(e * 4096 + c * ROWS + b + n, DEV, stride=2 * ROWS), :] for c in range(2)], axis=0
                    )
                    for n in range(2)
                ],
                axis=1,
            )
            value = dot_three(inner[0:256, :], inner[512:768, :], value)
            for n in range(2):
                middle[(b + n) * 256 : (b + n + 1) * 256, :] = value[:, n * LANES : (n + 1) * LANES]

        def filtered(t, _):
            at = pl.multiple_of(t * 8, 8)
            turns = [[turn[pl.ds(c * 2048 + b * DEV + at, 8), :] for c in range(2)] for b in range(ROWS)]
            value = [[middle[pl.ds(b * 256 + c * DEV + at, 8), :] for c in range(2)] for b in range(ROWS)]
            value = [value[0]] + [times(value[b], turns[b]) for b in range(1, ROWS)]
            value = sixteen(value, True)
            value = [
                times(value[q], [taps[pl.ds(c * 4096 + q * 256 + e + 2 * at, 8, stride=2), :] for c in range(2)])
                for q in range(ROWS)
            ]
            value = sixteen(value, False)
            value = [value[0]] + [times_conj(value[b], turns[b]) for b in range(1, ROWS)]
            for b in range(ROWS):
                for c in range(2):
                    middle[pl.ds(b * 256 + c * DEV + at, 8), :] = value[b][c]
            return 0

        lax.fori_loop(0, DEV // 8, filtered, 0)
        for b in range(0, ROWS, 2):
            value = jnp.concatenate([middle[(b + n) * 256 : (b + n + 1) * 256, :] for n in range(2)], axis=1)
            value = dot_three(inner[256:512, :], inner[768:1024, :], value)
            for n in range(2):
                for c in range(2):
                    send_three[pl.ds(e * 4096 + c * ROWS + b + n, DEV, stride=2 * ROWS), :] = value[
                        c * DEV : (c + 1) * DEV, n * LANES : (n + 1) * LANES
                    ]
        move_three.append(scatter(send_three, third, e * 4096, e * 4096, 2 * ROWS, 3 + e))

    arrive(move_three[0])
    arrive(move_three[1])
    scale = gain[0:1, :]
    for r in range(ROWS):
        value = first[pl.ds(r, DEV, stride=ROWS), :] * scale
        for c in range(2):
            at = (r * 2 + c) * DEV
            value += dot_three(
                back_high[at : at + DEV, :],
                back_low[at : at + DEV, :],
                third[pl.ds(c * ROWS + r, 256, stride=2 * ROWS), :],
            )
        send_four[pl.ds(r, DEV, stride=ROWS), :] = value
    move_four = scatter(send_four, mixed, 0, 0, ROWS, 5)
    arrive(move_four)
    for move in (move_one, *move_two, *move_three, move_four):
        move[0].wait_send()


def body(tokens, filter_spec, skip_gain):
    columns, across, inner, turn = tables()
    hbm = pl.BlockSpec(memory_space=pl.ANY)
    f32, bf16 = jnp.float32, jnp.bfloat16
    return pl.pallas_call(
        kernel,
        out_shape=jax.ShapeDtypeStruct((2048, LANES), f32),
        in_specs=[hbm, hbm, pl.BlockSpec(memory_space=pltpu.VMEM)] + [hbm] * 4,
        out_specs=hbm,
        scratch_shapes=[
            pltpu.VMEM((2048, LANES), f32),
            pltpu.VMEM((8192, LANES), f32),
            pltpu.VMEM((8192, LANES), f32),
            pltpu.VMEM((4096, LANES), f32),
            pltpu.VMEM((8192, LANES), f32),
            pltpu.VMEM((8192, LANES), f32),
            pltpu.VMEM((2048, LANES), f32),
            pltpu.VMEM((8192, LANES), bf16),
            pltpu.VMEM((8192, LANES), bf16),
            pltpu.VMEM((4096, 256), bf16),
            pltpu.VMEM((4096, 256), bf16),
            pltpu.VMEM((8192, LANES), f32),
            pltpu.VMEM(columns.shape, f32),
            pltpu.VMEM(across.shape, f32),
            pltpu.VMEM(inner.shape, bf16),
            pltpu.VMEM(turn.shape, f32),
            pltpu.SemaphoreType.DMA((6,)),
            pltpu.SemaphoreType.DMA((6,)),
            pltpu.SemaphoreType.DMA((14,)),
        ],
        compiler_params=pltpu.CompilerParams(
            collective_id=0, has_side_effects=True, vmem_limit_bytes=56 * 2**20
        ),
    )(
        tokens,
        filter_spec.reshape(8192, LANES),
        jnp.broadcast_to(skip_gain[None, :], (8, LANES)),
        jnp.asarray(columns),
        jnp.asarray(across),
        jnp.asarray(inner),
        jnp.asarray(turn),
    )


def solution(mesh):
    in_specs = (P(("loop", "grp"), None), P(None, None, ("loop", "grp"), None, None), P())
    out_specs = P(("loop", "grp"), None)
    return jax.shard_map(body, mesh=mesh, in_specs=in_specs, out_specs=out_specs, check_vma=False)
```

```python
import math

import jax
import jax.numpy as jnp
import numpy as np
from jax import lax
from jax.experimental import pallas as pl
from jax.experimental.pallas import tpu as pltpu
from jax.sharding import PartitionSpec as P

MESH = pl.DeviceIdType.MESH
DEV = 128
ROWS = 16
LANES = 128
FULL = 524288
STRIDE = 37


def split(value):
    high = value.astype(jnp.bfloat16)
    return high, (value - high.astype(jnp.float32)).astype(jnp.bfloat16)


def dot(a, b):
    return jnp.dot(a, b, preferred_element_type=jnp.float32)


def dot_three(a_high, a_low, b):
    b_high, b_low = split(b)
    return dot(a_high, b_high) + dot(a_high, b_low) + dot(a_low, b_high)


def dot_four(a_high, a_low, b):
    size = a_high.shape[0]
    value = dot(jnp.concatenate([a_high, a_low], axis=0), jnp.concatenate(split(b), axis=1))
    return (value[:size, :LANES] + value[:size, LANES:]) + (value[size:, :LANES] + value[size:, LANES:])


def roots(numerator, denominator):
    angles = -2.0 * math.pi * (np.asarray(numerator, np.int64) % denominator) / denominator
    return np.stack([np.cos(angles), np.sin(angles)])


def tables():
    row = np.arange(256)
    freq = 2 * (row % DEV) + row // DEV
    block = np.arange(DEV)
    base = roots(freq[:, None] * block[None, :], 256)
    shift = roots(freq[:, None] * block[None, :] * ROWS, FULL)
    step = np.broadcast_to(roots(freq, FULL)[:, :, None], (2, 256, LANES))
    columns = np.concatenate([base, shift, step]).reshape(6 * 256, LANES).astype(np.float32)
    base_t, shift_t = base.transpose(0, 2, 1), shift.transpose(0, 2, 1)
    step_t = np.broadcast_to(roots(freq, FULL)[:, None, :], (2, 8, 256))
    across = np.concatenate([t.reshape(-1, 256) for t in (base_t, shift_t, step_t)]).astype(np.float32)
    cos, sin = roots(block[:, None] * block[None, :], DEV)
    forward = np.block([[cos, -sin], [sin, cos]]).astype(np.float32)
    both = np.concatenate([forward, forward.T])
    both_high = both.astype(jnp.bfloat16)
    both_low = (both - both_high.astype(np.float32)).astype(jnp.bfloat16)
    inner = np.concatenate([both_high, both_low])
    turn = roots(np.arange(ROWS)[:, None] * block[None, :], 2048).reshape(2 * ROWS * DEV, 1)
    turn = np.broadcast_to(turn, (2 * ROWS * DEV, LANES)).astype(np.float32)
    return columns, across, inner, turn


def peer(loop, grp, i):
    k = (i * STRIDE) % DEV
    z = (loop // 2 + k // 16) % 4
    c = (loop + k // 64) % 2
    y = (grp // 4 + k // 4) % 4
    x = (grp + k) % 4
    return z * 2 + c, y * 4 + x


def times(a, b):
    return a[0] * b[0] - a[1] * b[1], a[0] * b[1] + a[1] * b[0]


def times_conj(a, b):
    return a[0] * b[0] + a[1] * b[1], a[1] * b[0] - a[0] * b[1]


def four(a, b, c, d, forward):
    s0, s1 = (a[0] + c[0], a[1] + c[1]), (a[0] - c[0], a[1] - c[1])
    s2, s3 = (b[0] + d[0], b[1] + d[1]), (b[0] - d[0], b[1] - d[1])
    s3 = (s3[1], -s3[0]) if forward else (-s3[1], s3[0])
    return (
        (s0[0] + s2[0], s0[1] + s2[1]),
        (s1[0] + s3[0], s1[1] + s3[1]),
        (s0[0] - s2[0], s0[1] - s2[1]),
        (s1[0] - s3[0], s1[1] - s3[1]),
    )


def sixteen(values, forward):
    sign = -1.0 if forward else 1.0
    parts = []
    for low in range(4):
        out = four(*[values[4 * high + low] for high in range(4)], forward)
        turned = []
        for k, v in enumerate(out):
            m = low * k
            if m == 0:
                turned.append(v)
            elif m == 4:
                turned.append((-sign * v[1], sign * v[0]))
            else:
                angle = sign * 2.0 * math.pi * m / 16
                turned.append(times(v, (math.cos(angle), math.sin(angle))))
        parts.append(turned)
    result = [None] * 16
    for k in range(4):
        out = four(*[parts[low][k] for low in range(4)], forward)
        for high in range(4):
            result[k + 4 * high] = out[high]
    return result


def kernel(
    tokens, taps_hbm, gain, columns_hbm, across_hbm, inner_hbm, turn_hbm, mixed,
    first, send_two, second, middle, send_three, third, send_four, total,
    out_high, out_low, back_high, back_low, taps, columns, across, inner, turn,
    send_sem, recv_sem, local_sem,
):
    loop = lax.axis_index("loop")
    grp = lax.axis_index("grp")
    me = loop * 16 + grp
    bar = pltpu.get_barrier_semaphore()

    def rows(start, size):
        return pl.ds(pl.multiple_of(start, 8), size)

    loads = [
        pltpu.make_async_copy(src, dst, local_sem.at[n])
        for n, (src, dst) in enumerate(
            ((columns_hbm, columns), (across_hbm, across), (inner_hbm, inner), (turn_hbm, turn), (taps_hbm, taps))
        )
    ]
    for load in loads:
        load.start()

    groups = [lax.rem(grp + n, 16) for n in range(16)]

    def greet(i, _):
        other = lax.rem(loop + i, 8)
        for group in groups:
            pl.semaphore_signal(bar, inc=1, device_id=(other, group), device_id_type=MESH)
        return 0

    for group in groups[1:]:
        pl.semaphore_signal(bar, inc=1, device_id=(loop, group), device_id_type=MESH)
    lax.fori_loop(1, 8, greet, 0)
    pl.semaphore_wait(bar, DEV - 1)

    def scatter(n, src, dst, size, src_at, dst_at):
        own = pltpu.make_async_copy(src.at[rows(src_at(me), size)], dst.at[rows(dst_at(me), size)], local_sem.at[5 + n])
        own.start()

        def send(i, _):
            l, g = peer(loop, grp, i)
            pltpu.make_async_remote_copy(
                src.at[rows(src_at(l * 16 + g), size)],
                dst.at[rows(dst_at(me), size)],
                send_sem.at[n],
                recv_sem.at[n],
                device_id=(l, g),
                device_id_type=MESH,
            ).start()
            return 0

        lax.fori_loop(1, DEV, send, 0)
        count = (DEV - 1) * size
        whole = pltpu.make_async_remote_copy(
            src.at[rows(0, count)],
            dst.at[rows(0, count)],
            send_sem.at[n],
            recv_sem.at[n],
            device_id=(loop, grp),
            device_id_type=MESH,
        )
        return whole, own

    def arrive(move):
        move[0].wait_recv()
        move[1].wait()

    def block(e, h, halves):
        if halves:
            return e * 4096 + h * 2048, 16
        return e * 4096 + h * 16, 32

    def strided(e, r, c, halves):
        base, stride = block(e, r // 8, halves)
        return pl.ds(base + c * 8 + r % 8, DEV, stride=stride)

    def exchange(n, src, dst, e, h, halves):
        base, stride = block(e, h, halves)
        at = lambda d: base + d * stride
        return scatter(n, src, dst, stride, at, at)

    move_one = [
        scatter(h, tokens, first, 8, lambda d: d * ROWS + h * 8, lambda d: h * 1024 + d * 8) for h in range(2)
    ]

    loads[0].wait()
    loads[1].wait()
    lane = lax.broadcasted_iota(jnp.int32, (16, LANES), 1)

    def build_out(t, _):
        at = pl.multiple_of(t * 16, 16)
        e, p = t // 8, pl.multiple_of((t % 8) * 16, 16)
        part = [columns[pl.ds(n * 256 + at, 16), :] for n in range(6)]
        shift = [jnp.sum(jnp.where(lane == me, v, 0.0), axis=1, keepdims=True) for v in part[2:4]]
        value = times(part[0:2], shift)
        for r in range(ROWS):
            for c in range(2):
                high, low = split(value[c])
                dst = pl.ds(((r * 2 + e) * 2 + c) * DEV + p, 16)
                out_high[dst, :] = high
                out_low[dst, :] = low
            if r < ROWS - 1:
                value = times(value, part[4:6])
        return 0

    lax.fori_loop(0, 16, build_out, 0)

    def build_back(t, _):
        at = pl.multiple_of(t * 16, 16)
        base = [across[pl.ds(n * DEV + at, 16), :] for n in range(2)]
        shift = [across[pl.ds((2 + n) * DEV + me, 1), :] for n in range(2)]
        step = [across[pl.ds(4 * DEV + n * 8, 1), :] for n in range(2)]
        value = times(base, shift)
        for r in range(ROWS):
            for c in range(2):
                high, low = split(value[c])
                for e in range(2):
                    dst = pl.ds((r * 2 + e) * DEV + at, 16)
                    back_high[dst, c * DEV : (c + 1) * DEV] = high[:, e * DEV : (e + 1) * DEV]
                    back_low[dst, c * DEV : (c + 1) * DEV] = low[:, e * DEV : (e + 1) * DEV]
            if r < ROWS - 1:
                value = times(value, step)
        return 0

    lax.fori_loop(0, 8, build_back, 0)

    def analyse(e, h):
        for r in range(8 * h, 8 * h + 8):
            at = (r * 2 + e) * 256
            value = dot_four(
                out_high[at : at + 256, :],
                out_low[at : at + 256, :],
                first[pl.ds(h * 1024 + r % 8, DEV, stride=8), :],
            )
            for c in range(2):
                send_two[strided(e, r, c, e == 0), :] = value[c * DEV : (c + 1) * DEV]

    arrive(move_one[0])
    analyse(0, 0)
    move_two = [exchange(2, send_two, second, 0, 0, True)]
    analyse(1, 0)
    arrive(move_one[1])
    analyse(0, 1)
    move_two.append(exchange(3, send_two, second, 0, 1, True))
    analyse(1, 1)
    move_two.append(exchange(4, send_two, second, 1, 0, False))

    for load in loads[2:]:
        load.wait()

    move_three = []
    for e in range(2):
        for move in move_two[2 * e : 2 * e + 2]:
            arrive(move)
        for b in range(0, ROWS, 2):
            value = jnp.concatenate(
                [
                    jnp.concatenate(
                        [second[strided(e, b + n, c, e == 0), :] for c in range(2)], axis=0
                    )
                    for n in range(2)
                ],
                axis=1,
            )
            value = dot_three(inner[0:256, :], inner[512:768, :], value)
            for n in range(2):
                middle[(b + n) * 256 : (b + n + 1) * 256, :] = value[:, n * LANES : (n + 1) * LANES]

        def filtered(t, _):
            at = pl.multiple_of(t * 8, 8)
            turns = [[turn[pl.ds(c * 2048 + b * DEV + at, 8), :] for c in range(2)] for b in range(ROWS)]
            value = [[middle[pl.ds(b * 256 + c * DEV + at, 8), :] for c in range(2)] for b in range(ROWS)]
            value = [value[0]] + [times(value[b], turns[b]) for b in range(1, ROWS)]
            value = sixteen(value, True)
            value = [
                times(value[q], [taps[pl.ds(c * 4096 + q * 256 + e + 2 * at, 8, stride=2), :] for c in range(2)])
                for q in range(ROWS)
            ]
            value = sixteen(value, False)
            value = [value[0]] + [times_conj(value[b], turns[b]) for b in range(1, ROWS)]
            for b in range(ROWS):
                for c in range(2):
                    middle[pl.ds(b * 256 + c * DEV + at, 8), :] = value[b][c]
            return 0

        lax.fori_loop(0, DEV // 8, filtered, 0)
        for b in range(0, ROWS, 2):
            value = jnp.concatenate([middle[(b + n) * 256 : (b + n + 1) * 256, :] for n in range(2)], axis=1)
            value = dot_three(inner[256:512, :], inner[768:1024, :], value)
            for n in range(2):
                for c in range(2):
                    send_three[strided(e, b + n, c, e == 1), :] = value[
                        c * DEV : (c + 1) * DEV, n * LANES : (n + 1) * LANES
                    ]
            if e == 1 and b == 6:
                move_three.append(exchange(6, send_three, third, 1, 0, True))
        move_three.append(exchange(5 + 2 * e, send_three, third, e, e, e == 1))

    def combine(e, r):
        at = (r * 2 + e) * DEV
        value = jnp.concatenate([third[strided(e, r, c, e == 1), :] for c in range(2)], axis=0)
        return dot_four(back_high[at : at + DEV, :], back_low[at : at + DEV, :], value)

    scale = gain[0:1, :] * float(FULL)
    arrive(move_three[0])
    for r in range(ROWS):
        direct = first[pl.ds(r // 8 * 1024 + r % 8, DEV, stride=8), :] * scale
        total[r * DEV : (r + 1) * DEV, :] = direct + combine(0, r)
    move_four = []
    for h in range(2):
        arrive(move_three[1 + h])
        for r in range(8 * h, 8 * h + 8):
            send_four[pl.ds(h * 1024 + r % 8, DEV, stride=8), :] = total[r * DEV : (r + 1) * DEV, :] + combine(1, r)
        move_four.append(
            scatter(8 + h, send_four, mixed, 8, lambda d: h * 1024 + d * 8, lambda d: d * ROWS + h * 8)
        )
    for move in move_four:
        arrive(move)
    for move in (*move_one, *move_two, *move_three, *move_four):
        move[0].wait_send()


def body(tokens, filter_spec, skip_gain):
    columns, across, inner, turn = tables()
    hbm = pl.BlockSpec(memory_space=pl.ANY)
    f32, bf16 = jnp.float32, jnp.bfloat16
    result = pl.pallas_call(
        kernel,
        out_shape=jax.ShapeDtypeStruct((2048, LANES), f32),
        in_specs=[hbm, hbm, pl.BlockSpec(memory_space=pltpu.VMEM)] + [hbm] * 4,
        out_specs=hbm,
        scratch_shapes=[
            pltpu.VMEM((2048, LANES), f32),
            pltpu.VMEM((8192, LANES), f32),
            pltpu.VMEM((8192, LANES), f32),
            pltpu.VMEM((4096, LANES), f32),
            pltpu.VMEM((8192, LANES), f32),
            pltpu.VMEM((8192, LANES), f32),
            pltpu.VMEM((2048, LANES), f32),
            pltpu.VMEM((2048, LANES), f32),
            pltpu.VMEM((8192, LANES), bf16),
            pltpu.VMEM((8192, LANES), bf16),
            pltpu.VMEM((4096, 256), bf16),
            pltpu.VMEM((4096, 256), bf16),
            pltpu.VMEM((8192, LANES), f32),
            pltpu.VMEM(columns.shape, f32),
            pltpu.VMEM(across.shape, f32),
            pltpu.VMEM(inner.shape, bf16),
            pltpu.VMEM(turn.shape, f32),
            pltpu.SemaphoreType.DMA((10,)),
            pltpu.SemaphoreType.DMA((10,)),
            pltpu.SemaphoreType.DMA((15,)),
        ],
        compiler_params=pltpu.CompilerParams(
            collective_id=0, has_side_effects=True, vmem_limit_bytes=56 * 2**20
        ),
    )(
        tokens,
        filter_spec.reshape(8192, LANES),
        skip_gain.reshape(1, LANES),
        jnp.asarray(columns),
        jnp.asarray(across),
        jnp.asarray(inner),
        jnp.asarray(turn),
    )
    return result * (1.0 / FULL)


def solution(mesh):
    in_specs = (P(("loop", "grp"), None), P(None, None, ("loop", "grp"), None, None), P())
    out_specs = P(("loop", "grp"), None)
    return jax.shard_map(body, mesh=mesh, in_specs=in_specs, out_specs=out_specs, check_vma=False)
```

```python
import math

import jax
import jax.numpy as jnp
import numpy as np
from jax import lax
from jax.experimental import pallas as pl
from jax.experimental.pallas import tpu as pltpu
from jax.sharding import PartitionSpec as P

MESH = pl.DeviceIdType.MESH
DEV = 128
ROWS = 16
LANES = 128
FULL = 524288
STRIDE = 37


def split(value):
    high = value.astype(jnp.bfloat16)
    return high, (value - high.astype(jnp.float32)).astype(jnp.bfloat16)


def dot(a, b):
    return jnp.dot(a, b, preferred_element_type=jnp.float32)


def dot_three(a_high, a_low, b):
    b_high, b_low = split(b)
    return dot(a_high, b_high) + dot(a_high, b_low) + dot(a_low, b_high)


def dot_four(a_high, a_low, b):
    size = a_high.shape[0]
    value = dot(jnp.concatenate([a_high, a_low], axis=0), jnp.concatenate(split(b), axis=1))
    return (value[:size, :LANES] + value[:size, LANES:]) + (value[size:, :LANES] + value[size:, LANES:])


def roots(numerator, denominator):
    angles = -2.0 * math.pi * (np.asarray(numerator, np.int64) % denominator) / denominator
    return np.stack([np.cos(angles), np.sin(angles)])


def tables():
    row = np.arange(256)
    freq = 2 * (row % DEV) + row // DEV
    block = np.arange(DEV)
    base = roots(freq[:, None] * block[None, :], 256)
    shift = roots(freq[:, None] * block[None, :] * ROWS, FULL)
    step = np.broadcast_to(roots(freq, FULL)[:, :, None], (2, 256, LANES))
    columns = np.concatenate([base, shift, step]).reshape(6 * 256, LANES).astype(np.float32)
    base_t, shift_t = base.transpose(0, 2, 1), shift.transpose(0, 2, 1)
    step_t = np.broadcast_to(roots(freq, FULL)[:, None, :], (2, 8, 256))
    across = np.concatenate([t.reshape(-1, 256) for t in (base_t, shift_t, step_t)]).astype(np.float32)
    cos, sin = roots(block[:, None] * block[None, :], DEV)
    forward = np.block([[cos, -sin], [sin, cos]]).astype(np.float32)
    both = np.concatenate([forward, forward.T])
    both_high = both.astype(jnp.bfloat16)
    both_low = (both - both_high.astype(np.float32)).astype(jnp.bfloat16)
    inner = np.concatenate([both_high, both_low])
    turn = roots(np.arange(ROWS)[:, None] * block[None, :], 2048).reshape(2 * ROWS * DEV, 1)
    turn = np.broadcast_to(turn, (2 * ROWS * DEV, LANES)).astype(np.float32)
    return columns, across, inner, turn


def peer(loop, grp, i):
    k = lax.rem(i * STRIDE, DEV)
    z = lax.rem(lax.div(loop, 2) + lax.div(k, 16), 4)
    c = lax.rem(loop + lax.div(k, 64), 2)
    y = lax.rem(lax.div(grp, 4) + lax.div(k, 4), 4)
    x = lax.rem(grp + k, 4)
    return z * 2 + c, y * 4 + x


def times(a, b):
    return a[0] * b[0] - a[1] * b[1], a[0] * b[1] + a[1] * b[0]


def times_conj(a, b):
    return a[0] * b[0] + a[1] * b[1], a[1] * b[0] - a[0] * b[1]


def four(a, b, c, d, forward):
    s0, s1 = (a[0] + c[0], a[1] + c[1]), (a[0] - c[0], a[1] - c[1])
    s2, s3 = (b[0] + d[0], b[1] + d[1]), (b[0] - d[0], b[1] - d[1])
    s3 = (s3[1], -s3[0]) if forward else (-s3[1], s3[0])
    return (
        (s0[0] + s2[0], s0[1] + s2[1]),
        (s1[0] + s3[0], s1[1] + s3[1]),
        (s0[0] - s2[0], s0[1] - s2[1]),
        (s1[0] - s3[0], s1[1] - s3[1]),
    )


def sixteen(values, forward):
    sign = -1.0 if forward else 1.0
    parts = []
    for low in range(4):
        out = four(*[values[4 * high + low] for high in range(4)], forward)
        turned = []
        for k, v in enumerate(out):
            m = low * k
            if m == 0:
                turned.append(v)
            elif m == 4:
                turned.append((-sign * v[1], sign * v[0]))
            else:
                angle = sign * 2.0 * math.pi * m / 16
                turned.append(times(v, (math.cos(angle), math.sin(angle))))
        parts.append(turned)
    result = [None] * 16
    for k in range(4):
        out = four(*[parts[low][k] for low in range(4)], forward)
        for high in range(4):
            result[k + 4 * high] = out[high]
    return result


def kernel(
    tokens, taps_hbm, columns_hbm, across_hbm, inner_hbm, turn_hbm, mixed,
    first, send_two, second, middle, send_three, third, send_four, total,
    out_high, out_low, back_high, back_low, taps, columns, across, inner, turn,
    send_sem, recv_sem, local_sem,
):
    loop = lax.axis_index("loop")
    grp = lax.axis_index("grp")
    me = loop * 16 + grp
    bar = pltpu.get_barrier_semaphore()

    def rows(start, size):
        return pl.ds(pl.multiple_of(start, 8), size)

    loads = [
        pltpu.make_async_copy(src, dst, local_sem.at[n])
        for n, (src, dst) in enumerate(
            ((columns_hbm, columns), (across_hbm, across), (inner_hbm, inner), (turn_hbm, turn), (taps_hbm, taps))
        )
    ]
    for load in loads[:2]:
        load.start()

    groups = [lax.rem(grp + n, 16) for n in range(16)]

    def greet(i, _):
        other = lax.rem(loop + i, 8)
        for group in groups:
            pl.semaphore_signal(bar, inc=1, device_id=(other, group), device_id_type=MESH)
        return 0

    for group in groups[1:]:
        pl.semaphore_signal(bar, inc=1, device_id=(loop, group), device_id_type=MESH)
    lax.fori_loop(1, 8, greet, 0)
    pl.semaphore_wait(bar, DEV - 1)

    def scatter(n, src, dst, size, src_at, dst_at):
        own = pltpu.make_async_copy(src.at[rows(src_at(me), size)], dst.at[rows(dst_at(me), size)], local_sem.at[5 + n])
        own.start()

        def send(i):
            l, g = peer(loop, grp, i)
            pltpu.make_async_remote_copy(
                src.at[rows(src_at(l * 16 + g), size)],
                dst.at[rows(dst_at(me), size)],
                send_sem.at[n],
                recv_sem.at[n],
                device_id=(l, g),
                device_id_type=MESH,
            ).start()

        def send_three(t, _):
            for u in range(3):
                send(2 + 3 * t + u)
            return 0

        send(1)
        lax.fori_loop(0, (DEV - 2) // 3, send_three, 0)
        count = (DEV - 1) * size
        whole = pltpu.make_async_remote_copy(
            src.at[rows(0, count)],
            dst.at[rows(0, count)],
            send_sem.at[n],
            recv_sem.at[n],
            device_id=(loop, grp),
            device_id_type=MESH,
        )
        return whole, own

    def arrive(move):
        move[0].wait_recv()
        move[1].wait()

    def block(e, h, halves):
        if halves:
            return e * 4096 + h * 2048, 16
        return e * 4096 + h * 16, 32

    def strided(e, r, c, halves):
        base, stride = block(e, r // 8, halves)
        return pl.ds(base + c * 8 + r % 8, DEV, stride=stride)

    def exchange(n, src, dst, e, h, halves):
        base, stride = block(e, h, halves)
        at = lambda d: base + d * stride
        return scatter(n, src, dst, stride, at, at)

    move_one = [
        scatter(h, tokens, first, 8, lambda d: d * ROWS + h * 8, lambda d: h * 1024 + d * 8) for h in range(2)
    ]

    for load in loads[2:]:
        load.start()
    loads[0].wait()
    loads[1].wait()
    lane = lax.broadcasted_iota(jnp.int32, (16, LANES), 1)

    def build_out(t, _):
        at = pl.multiple_of(t * 16, 16)
        e, p = t // 8, pl.multiple_of((t % 8) * 16, 16)
        part = [columns[pl.ds(n * 256 + at, 16), :] for n in range(6)]
        shift = [jnp.sum(jnp.where(lane == me, v, 0.0), axis=1, keepdims=True) for v in part[2:4]]
        value = times(part[0:2], shift)
        for r in range(ROWS):
            for c in range(2):
                high, low = split(value[c])
                dst = pl.ds(((r * 2 + e) * 2 + c) * DEV + p, 16)
                out_high[dst, :] = high
                out_low[dst, :] = low
            if r < ROWS - 1:
                value = times(value, part[4:6])
        return 0

    lax.fori_loop(0, 16, build_out, 0)

    def build_back(t, _):
        at = pl.multiple_of(t * 16, 16)
        base = [across[pl.ds(n * DEV + at, 16), :] for n in range(2)]
        shift = [across[pl.ds((2 + n) * DEV + me, 1), :] for n in range(2)]
        step = [across[pl.ds(4 * DEV + n * 8, 1), :] for n in range(2)]
        value = times(base, shift)
        for r in range(ROWS):
            for c in range(2):
                high, low = split(value[c])
                for e in range(2):
                    dst = pl.ds((r * 2 + e) * DEV + at, 16)
                    back_high[dst, c * DEV : (c + 1) * DEV] = high[:, e * DEV : (e + 1) * DEV]
                    back_low[dst, c * DEV : (c + 1) * DEV] = low[:, e * DEV : (e + 1) * DEV]
            if r < ROWS - 1:
                value = times(value, step)
        return 0

    lax.fori_loop(0, 8, build_back, 0)

    def analyse(e, h):
        for r in range(8 * h, 8 * h + 8):
            at = (r * 2 + e) * 256
            value = dot_four(
                out_high[at : at + 256, :],
                out_low[at : at + 256, :],
                first[pl.ds(h * 1024 + r % 8, DEV, stride=8), :],
            )
            for c in range(2):
                send_two[strided(e, r, c, e == 0), :] = value[c * DEV : (c + 1) * DEV]

    arrive(move_one[0])
    analyse(0, 0)
    move_two = [exchange(2, send_two, second, 0, 0, True)]
    analyse(1, 0)
    arrive(move_one[1])
    analyse(0, 1)
    move_two.append(exchange(3, send_two, second, 0, 1, True))
    analyse(1, 1)
    move_two.append(exchange(4, send_two, second, 1, 0, False))

    for load in loads[2:]:
        load.wait()

    move_three = []
    for e in range(2):
        for move in move_two[2 * e : 2 * e + 2]:
            arrive(move)
        for b in range(0, ROWS, 2):
            value = jnp.concatenate(
                [
                    jnp.concatenate(
                        [second[strided(e, b + n, c, e == 0), :] for c in range(2)], axis=0
                    )
                    for n in range(2)
                ],
                axis=1,
            )
            value = dot_three(inner[0:256, :], inner[512:768, :], value)
            for n in range(2):
                middle[(b + n) * 256 : (b + n + 1) * 256, :] = value[:, n * LANES : (n + 1) * LANES]

        def filtered(t, _):
            at = pl.multiple_of(t * 8, 8)
            turns = [[turn[pl.ds(c * 2048 + b * DEV + at, 8), :] for c in range(2)] for b in range(ROWS)]
            value = [[middle[pl.ds(b * 256 + c * DEV + at, 8), :] for c in range(2)] for b in range(ROWS)]
            value = [value[0]] + [times(value[b], turns[b]) for b in range(1, ROWS)]
            value = sixteen(value, True)
            value = [
                times(value[q], [taps[pl.ds(c * 4096 + q * 256 + e + 2 * at, 8, stride=2), :] for c in range(2)])
                for q in range(ROWS)
            ]
            value = sixteen(value, False)
            value = [value[0]] + [times_conj(value[b], turns[b]) for b in range(1, ROWS)]
            for b in range(ROWS):
                for c in range(2):
                    middle[pl.ds(b * 256 + c * DEV + at, 8), :] = value[b][c]
            return 0

        lax.fori_loop(0, DEV // 8, filtered, 0)
        for b in range(0, ROWS, 2):
            value = jnp.concatenate([middle[(b + n) * 256 : (b + n + 1) * 256, :] for n in range(2)], axis=1)
            value = dot_three(inner[256:512, :], inner[768:1024, :], value)
            for n in range(2):
                for c in range(2):
                    send_three[strided(e, b + n, c, e == 1), :] = value[
                        c * DEV : (c + 1) * DEV, n * LANES : (n + 1) * LANES
                    ]
            if e == 1 and b == 6:
                move_three.append(exchange(6, send_three, third, 1, 0, True))
        move_three.append(exchange(5 + 2 * e, send_three, third, e, e, e == 1))

    def combine(e, r):
        at = (r * 2 + e) * DEV
        value = jnp.concatenate([third[strided(e, r, c, e == 1), :] for c in range(2)], axis=0)
        return dot_four(back_high[at : at + DEV, :], back_low[at : at + DEV, :], value)

    arrive(move_three[0])
    for r in range(ROWS):
        total[r * DEV : (r + 1) * DEV, :] = combine(0, r)
    move_four = []
    for h in range(2):
        arrive(move_three[1 + h])
        for r in range(8 * h, 8 * h + 8):
            send_four[pl.ds(h * 1024 + r % 8, DEV, stride=8), :] = total[r * DEV : (r + 1) * DEV, :] + combine(1, r)
        move_four.append(
            scatter(8 + h, send_four, mixed, 8, lambda d: h * 1024 + d * 8, lambda d: d * ROWS + h * 8)
        )
    for move in move_four:
        arrive(move)
    for move in (*move_one, *move_two, *move_three, *move_four):
        move[0].wait_send()


def body(tokens, filter_spec, skip_gain):
    columns, across, inner, turn = tables()
    hbm = pl.BlockSpec(memory_space=pl.ANY)
    f32, bf16 = jnp.float32, jnp.bfloat16
    result = pl.pallas_call(
        kernel,
        out_shape=jax.ShapeDtypeStruct((2048, LANES), f32),
        in_specs=[hbm] * 6,
        out_specs=hbm,
        scratch_shapes=[
            pltpu.VMEM((2048, LANES), f32),
            pltpu.VMEM((8192, LANES), f32),
            pltpu.VMEM((8192, LANES), f32),
            pltpu.VMEM((4096, LANES), f32),
            pltpu.VMEM((8192, LANES), f32),
            pltpu.VMEM((8192, LANES), f32),
            pltpu.VMEM((2048, LANES), f32),
            pltpu.VMEM((2048, LANES), f32),
            pltpu.VMEM((8192, LANES), bf16),
            pltpu.VMEM((8192, LANES), bf16),
            pltpu.VMEM((4096, 256), bf16),
            pltpu.VMEM((4096, 256), bf16),
            pltpu.VMEM((8192, LANES), f32),
            pltpu.VMEM(columns.shape, f32),
            pltpu.VMEM(across.shape, f32),
            pltpu.VMEM(inner.shape, bf16),
            pltpu.VMEM(turn.shape, f32),
            pltpu.SemaphoreType.DMA((10,)),
            pltpu.SemaphoreType.DMA((10,)),
            pltpu.SemaphoreType.DMA((15,)),
        ],
        compiler_params=pltpu.CompilerParams(
            collective_id=0, has_side_effects=True, vmem_limit_bytes=56 * 2**20
        ),
    )(
        tokens,
        filter_spec.reshape(8192, LANES),
        jnp.asarray(columns),
        jnp.asarray(across),
        jnp.asarray(inner),
        jnp.asarray(turn),
    )
    return result * (1.0 / FULL) + skip_gain[None, :] * tokens


def solution(mesh):
    in_specs = (P(("loop", "grp"), None), P(None, None, ("loop", "grp"), None, None), P())
    out_specs = P(("loop", "grp"), None)
    return jax.shard_map(body, mesh=mesh, in_specs=in_specs, out_specs=out_specs, check_vma=False)
```

```python
import math

import jax
import jax.numpy as jnp
import numpy as np
from jax import lax
from jax.experimental import pallas as pl
from jax.experimental.pallas import tpu as pltpu
from jax.sharding import PartitionSpec as P

MESH = pl.DeviceIdType.MESH
DEV = 128
ROWS = 16
LANES = 128
FULL = 524288
STRIDE = 101


def split(value):
    high = value.astype(jnp.bfloat16)
    return high, (value - high.astype(jnp.float32)).astype(jnp.bfloat16)


def dot(a, b):
    return jnp.dot(a, b, preferred_element_type=jnp.float32)


def dot_three(a_high, a_low, b):
    b_high, b_low = split(b)
    return dot(a_high, b_high) + dot(a_high, b_low) + dot(a_low, b_high)


def dot_four(a_high, a_low, b):
    size = a_high.shape[0]
    value = dot(jnp.concatenate([a_high, a_low], axis=0), jnp.concatenate(split(b), axis=1))
    return (value[:size, :LANES] + value[:size, LANES:]) + (value[size:, :LANES] + value[size:, LANES:])


def roots(numerator, denominator):
    angles = -2.0 * math.pi * (np.asarray(numerator, np.int64) % denominator) / denominator
    return np.stack([np.cos(angles), np.sin(angles)])


def tables():
    row = np.arange(256)
    freq = 2 * (row % DEV) + row // DEV
    block = np.arange(DEV)
    base = roots(freq[:, None] * block[None, :], 256)
    shift = roots(freq[:, None] * block[None, :] * ROWS, FULL)
    step = np.broadcast_to(roots(freq, FULL)[:, :, None], (2, 256, LANES))
    columns = np.concatenate([base, shift, step]).reshape(6 * 256, LANES).astype(np.float32)
    base_t, shift_t = base.transpose(0, 2, 1), shift.transpose(0, 2, 1)
    step_t = np.broadcast_to(roots(freq, FULL)[:, None, :], (2, 8, 256))
    across = np.concatenate([t.reshape(-1, 256) for t in (base_t, shift_t, step_t)]).astype(np.float32)
    cos, sin = roots(block[:, None] * block[None, :], DEV)
    forward = np.block([[cos, -sin], [sin, cos]]).astype(np.float32)
    both = np.concatenate([forward, forward.T])
    both_high = both.astype(jnp.bfloat16)
    both_low = (both - both_high.astype(np.float32)).astype(jnp.bfloat16)
    inner = np.concatenate([both_high, both_low])
    turn = roots(np.arange(ROWS)[:, None] * block[None, :], 2048).reshape(2 * ROWS * DEV, 1)
    turn = np.broadcast_to(turn, (2 * ROWS * DEV, LANES)).astype(np.float32)
    return columns, across, inner, turn


def peer(loop, grp, i):
    k = lax.rem(i * STRIDE, DEV)
    z = lax.rem(lax.div(loop, 2) + lax.div(k, 16), 4)
    c = lax.rem(loop + lax.div(k, 64), 2)
    y = lax.rem(lax.div(grp, 4) + lax.div(k, 4), 4)
    x = lax.rem(grp + k, 4)
    return z * 2 + c, y * 4 + x


def times(a, b):
    return a[0] * b[0] - a[1] * b[1], a[0] * b[1] + a[1] * b[0]


def times_conj(a, b):
    return a[0] * b[0] + a[1] * b[1], a[1] * b[0] - a[0] * b[1]


def four(a, b, c, d, forward):
    s0, s1 = (a[0] + c[0], a[1] + c[1]), (a[0] - c[0], a[1] - c[1])
    s2, s3 = (b[0] + d[0], b[1] + d[1]), (b[0] - d[0], b[1] - d[1])
    s3 = (s3[1], -s3[0]) if forward else (-s3[1], s3[0])
    return (
        (s0[0] + s2[0], s0[1] + s2[1]),
        (s1[0] + s3[0], s1[1] + s3[1]),
        (s0[0] - s2[0], s0[1] - s2[1]),
        (s1[0] - s3[0], s1[1] - s3[1]),
    )


def sixteen(values, forward):
    sign = -1.0 if forward else 1.0
    parts = []
    for low in range(4):
        out = four(*[values[4 * high + low] for high in range(4)], forward)
        turned = []
        for k, v in enumerate(out):
            m = low * k
            if m == 0:
                turned.append(v)
            elif m == 4:
                turned.append((-sign * v[1], sign * v[0]))
            else:
                angle = sign * 2.0 * math.pi * m / 16
                turned.append(times(v, (math.cos(angle), math.sin(angle))))
        parts.append(turned)
    result = [None] * 16
    for k in range(4):
        out = four(*[parts[low][k] for low in range(4)], forward)
        for high in range(4):
            result[k + 4 * high] = out[high]
    return result


def kernel(
    tokens, taps_hbm, columns_hbm, across_hbm, inner_hbm, turn_hbm, mixed,
    first, send_two, second, middle, send_three, third, send_four, total,
    out_high, out_low, back_high, back_low, taps, columns, across, inner, turn,
    send_sem, recv_sem, local_sem,
):
    loop = lax.axis_index("loop")
    grp = lax.axis_index("grp")
    me = loop * 16 + grp
    bar = pltpu.get_barrier_semaphore()

    def rows(start, size):
        return pl.ds(pl.multiple_of(start, 8), size)

    loads = [
        pltpu.make_async_copy(src, dst, local_sem.at[n])
        for n, (src, dst) in enumerate(
            ((columns_hbm, columns), (across_hbm, across), (inner_hbm, inner), (turn_hbm, turn), (taps_hbm, taps))
        )
    ]
    for load in loads[:2]:
        load.start()

    groups = [lax.rem(grp + n, 16) for n in range(16)]

    def greet(i, _):
        other = lax.rem(loop + i, 8)
        for group in groups:
            pl.semaphore_signal(bar, inc=1, device_id=(other, group), device_id_type=MESH)
        return 0

    for group in groups[1:]:
        pl.semaphore_signal(bar, inc=1, device_id=(loop, group), device_id_type=MESH)
    lax.fori_loop(1, 8, greet, 0)
    pl.semaphore_wait(bar, DEV - 1)

    def scatter(n, src, dst, size, src_at, dst_at):
        own = pltpu.make_async_copy(src.at[rows(src_at(me), size)], dst.at[rows(dst_at(me), size)], local_sem.at[5 + n])
        own.start()

        def send(i):
            l, g = peer(loop, grp, i)
            pltpu.make_async_remote_copy(
                src.at[rows(src_at(l * 16 + g), size)],
                dst.at[rows(dst_at(me), size)],
                send_sem.at[n],
                recv_sem.at[n],
                device_id=(l, g),
                device_id_type=MESH,
            ).start()

        def send_three(t, _):
            for u in range(3):
                send(2 + 3 * t + u)
            return 0

        send(1)
        lax.fori_loop(0, (DEV - 2) // 3, send_three, 0)
        count = (DEV - 1) * size
        whole = pltpu.make_async_remote_copy(
            src.at[rows(0, count)],
            dst.at[rows(0, count)],
            send_sem.at[n],
            recv_sem.at[n],
            device_id=(loop, grp),
            device_id_type=MESH,
        )
        return whole, own

    def arrive(move):
        move[0].wait_recv()
        move[1].wait()

    def block(e, h, halves):
        if halves:
            return e * 4096 + h * 2048, 16
        return e * 4096 + h * 16, 32

    def strided(e, r, c, halves):
        base, stride = block(e, r // 8, halves)
        return pl.ds(base + c * 8 + r % 8, DEV, stride=stride)

    def exchange(n, src, dst, e, h, halves):
        base, stride = block(e, h, halves)
        at = lambda d: base + d * stride
        return scatter(n, src, dst, stride, at, at)

    move_one = [
        scatter(h, tokens, first, 8, lambda d: d * ROWS + h * 8, lambda d: h * 1024 + d * 8) for h in range(2)
    ]

    for load in loads[2:]:
        load.start()
    loads[0].wait()
    loads[1].wait()
    lane = lax.broadcasted_iota(jnp.int32, (16, LANES), 1)

    def build_out(t, _):
        at = pl.multiple_of(t * 16, 16)
        e, p = t // 8, pl.multiple_of((t % 8) * 16, 16)
        part = [columns[pl.ds(n * 256 + at, 16), :] for n in range(6)]
        shift = [jnp.sum(jnp.where(lane == me, v, 0.0), axis=1, keepdims=True) for v in part[2:4]]
        value = times(part[0:2], shift)
        for r in range(ROWS):
            for c in range(2):
                high, low = split(value[c])
                dst = pl.ds(((r * 2 + e) * 2 + c) * DEV + p, 16)
                out_high[dst, :] = high
                out_low[dst, :] = low
            if r < ROWS - 1:
                value = times(value, part[4:6])
        return 0

    lax.fori_loop(0, 16, build_out, 0)

    def build_back(t, _):
        at = pl.multiple_of(t * 16, 16)
        base = [across[pl.ds(n * DEV + at, 16), :] for n in range(2)]
        shift = [across[pl.ds((2 + n) * DEV + me, 1), :] for n in range(2)]
        step = [across[pl.ds(4 * DEV + n * 8, 1), :] for n in range(2)]
        value = times(base, shift)
        for r in range(ROWS):
            for c in range(2):
                high, low = split(value[c])
                for e in range(2):
                    dst = pl.ds((r * 2 + e) * DEV + at, 16)
                    back_high[dst, c * DEV : (c + 1) * DEV] = high[:, e * DEV : (e + 1) * DEV]
                    back_low[dst, c * DEV : (c + 1) * DEV] = low[:, e * DEV : (e + 1) * DEV]
            if r < ROWS - 1:
                value = times(value, step)
        return 0

    lax.fori_loop(0, 8, build_back, 0)

    def analyse(e, h):
        for r in range(8 * h, 8 * h + 8):
            at = (r * 2 + e) * 256
            value = dot_four(
                out_high[at : at + 256, :],
                out_low[at : at + 256, :],
                first[pl.ds(h * 1024 + r % 8, DEV, stride=8), :],
            )
            for c in range(2):
                send_two[strided(e, r, c, e == 0), :] = value[c * DEV : (c + 1) * DEV]

    arrive(move_one[0])
    analyse(0, 0)
    move_two = [exchange(2, send_two, second, 0, 0, True)]
    analyse(1, 0)
    arrive(move_one[1])
    analyse(0, 1)
    move_two.append(exchange(3, send_two, second, 0, 1, True))
    analyse(1, 1)
    move_two.append(exchange(4, send_two, second, 1, 0, False))

    for load in loads[2:]:
        load.wait()

    move_three = []
    for e in range(2):
        for move in move_two[2 * e : 2 * e + 2]:
            arrive(move)
        for b in range(0, ROWS, 2):
            value = jnp.concatenate(
                [
                    jnp.concatenate(
                        [second[strided(e, b + n, c, e == 0), :] for c in range(2)], axis=0
                    )
                    for n in range(2)
                ],
                axis=1,
            )
            value = dot_three(inner[0:256, :], inner[512:768, :], value)
            for n in range(2):
                middle[(b + n) * 256 : (b + n + 1) * 256, :] = value[:, n * LANES : (n + 1) * LANES]

        def filtered(t, _):
            at = pl.multiple_of(t * 8, 8)
            turns = [[turn[pl.ds(c * 2048 + b * DEV + at, 8), :] for c in range(2)] for b in range(ROWS)]
            value = [[middle[pl.ds(b * 256 + c * DEV + at, 8), :] for c in range(2)] for b in range(ROWS)]
            value = [value[0]] + [times(value[b], turns[b]) for b in range(1, ROWS)]
            value = sixteen(value, True)
            value = [
                times(value[q], [taps[pl.ds(c * 4096 + q * 256 + e + 2 * at, 8, stride=2), :] for c in range(2)])
                for q in range(ROWS)
            ]
            value = sixteen(value, False)
            value = [value[0]] + [times_conj(value[b], turns[b]) for b in range(1, ROWS)]
            for b in range(ROWS):
                for c in range(2):
                    middle[pl.ds(b * 256 + c * DEV + at, 8), :] = value[b][c]
            return 0

        lax.fori_loop(0, DEV // 8, filtered, 0)
        for b in range(0, ROWS, 2):
            value = jnp.concatenate([middle[(b + n) * 256 : (b + n + 1) * 256, :] for n in range(2)], axis=1)
            value = dot_three(inner[256:512, :], inner[768:1024, :], value)
            for n in range(2):
                for c in range(2):
                    send_three[strided(e, b + n, c, e == 1), :] = value[
                        c * DEV : (c + 1) * DEV, n * LANES : (n + 1) * LANES
                    ]
            if e == 1 and b == 6:
                move_three.append(exchange(6, send_three, third, 1, 0, True))
        move_three.append(exchange(5 + 2 * e, send_three, third, e, e, e == 1))

    def combine(e, r):
        at = (r * 2 + e) * DEV
        value = jnp.concatenate([third[strided(e, r, c, e == 1), :] for c in range(2)], axis=0)
        return dot_four(back_high[at : at + DEV, :], back_low[at : at + DEV, :], value)

    arrive(move_three[0])
    for r in range(ROWS):
        total[r * DEV : (r + 1) * DEV, :] = combine(0, r)
    move_four = []
    for h in range(2):
        arrive(move_three[1 + h])
        for r in range(8 * h, 8 * h + 8):
            send_four[pl.ds(h * 1024 + r % 8, DEV, stride=8), :] = total[r * DEV : (r + 1) * DEV, :] + combine(1, r)
        move_four.append(
            scatter(8 + h, send_four, mixed, 8, lambda d: h * 1024 + d * 8, lambda d: d * ROWS + h * 8)
        )
    for move in move_four:
        arrive(move)
    for move in (*move_one, *move_two, *move_three, *move_four):
        move[0].wait_send()


def body(tokens, filter_spec, skip_gain):
    columns, across, inner, turn = tables()
    hbm = pl.BlockSpec(memory_space=pl.ANY)
    f32, bf16 = jnp.float32, jnp.bfloat16
    result = pl.pallas_call(
        kernel,
        out_shape=jax.ShapeDtypeStruct((2048, LANES), f32),
        in_specs=[hbm] * 6,
        out_specs=hbm,
        scratch_shapes=[
            pltpu.VMEM((2048, LANES), f32),
            pltpu.VMEM((8192, LANES), f32),
            pltpu.VMEM((8192, LANES), f32),
            pltpu.VMEM((4096, LANES), f32),
            pltpu.VMEM((8192, LANES), f32),
            pltpu.VMEM((8192, LANES), f32),
            pltpu.VMEM((2048, LANES), f32),
            pltpu.VMEM((2048, LANES), f32),
            pltpu.VMEM((8192, LANES), bf16),
            pltpu.VMEM((8192, LANES), bf16),
            pltpu.VMEM((4096, 256), bf16),
            pltpu.VMEM((4096, 256), bf16),
            pltpu.VMEM((8192, LANES), f32),
            pltpu.VMEM(columns.shape, f32),
            pltpu.VMEM(across.shape, f32),
            pltpu.VMEM(inner.shape, bf16),
            pltpu.VMEM(turn.shape, f32),
            pltpu.SemaphoreType.DMA((10,)),
            pltpu.SemaphoreType.DMA((10,)),
            pltpu.SemaphoreType.DMA((15,)),
        ],
        compiler_params=pltpu.CompilerParams(
            collective_id=0, has_side_effects=True, vmem_limit_bytes=56 * 2**20
        ),
    )(
        tokens,
        filter_spec.reshape(8192, LANES),
        jnp.asarray(columns),
        jnp.asarray(across),
        jnp.asarray(inner),
        jnp.asarray(turn),
    )
    return result * (1.0 / FULL) + skip_gain[None, :] * tokens


def solution(mesh):
    in_specs = (P(("loop", "grp"), None), P(None, None, ("loop", "grp"), None, None), P())
    out_specs = P(("loop", "grp"), None)
    return jax.shard_map(body, mesh=mesh, in_specs=in_specs, out_specs=out_specs, check_vma=False)
```

```python
import math

import jax
import jax.numpy as jnp
import numpy as np
from jax import lax
from jax.experimental import pallas as pl
from jax.experimental.pallas import tpu as pltpu
from jax.sharding import PartitionSpec as P

MESH = pl.DeviceIdType.MESH
DEV = 128
ROWS = 16
LANES = 128
FULL = 524288
PAD = 32
STRIDE = 101


def split(value):
    high = value.astype(jnp.bfloat16)
    return high, (value - high.astype(jnp.float32)).astype(jnp.bfloat16)


def dot(a, b):
    return jnp.dot(a, b, preferred_element_type=jnp.float32)


def dot_three(a_high, a_low, b):
    b_high, b_low = split(b)
    return dot(a_high, b_high) + dot(a_high, b_low) + dot(a_low, b_high)


def dot_four(a_high, a_low, b):
    size = a_high.shape[0]
    value = dot(jnp.concatenate([a_high, a_low], axis=0), jnp.concatenate(split(b), axis=1))
    return (value[:size, :LANES] + value[:size, LANES:]) + (value[size:, :LANES] + value[size:, LANES:])


def roots(numerator, denominator):
    angles = -2.0 * math.pi * (np.asarray(numerator, np.int64) % denominator) / denominator
    return np.stack([np.cos(angles), np.sin(angles)])


def tables():
    row = np.arange(256)
    freq = 2 * (row % DEV) + row // DEV
    block = np.arange(DEV)
    base = roots(freq[:, None] * block[None, :], 256)
    shift = roots(freq[:, None] * block[None, :] * ROWS, FULL)
    step = np.broadcast_to(roots(freq, FULL)[:, :, None], (2, 256, LANES))
    columns = np.concatenate([base, shift, step]).reshape(6 * 256, LANES).astype(np.float32)
    base_t, shift_t = base.transpose(0, 2, 1), shift.transpose(0, 2, 1)
    step_t = np.broadcast_to(roots(freq, FULL)[:, None, :], (2, 8, 256))
    across = np.concatenate([t.reshape(-1, 256) for t in (base_t, shift_t, step_t)]).astype(np.float32)
    cos, sin = roots(block[:, None] * block[None, :], DEV)
    forward = np.block([[cos, -sin], [sin, cos]]).astype(np.float32)
    both = np.concatenate([forward, forward.T])
    both_high = both.astype(jnp.bfloat16)
    both_low = (both - both_high.astype(np.float32)).astype(jnp.bfloat16)
    inner = np.concatenate([both_high, both_low])
    turn = roots(np.arange(ROWS)[:, None] * block[None, :], 2048).reshape(2 * ROWS * DEV, 1)
    turn = np.broadcast_to(turn, (2 * ROWS * DEV, LANES)).astype(np.float32)
    return columns, across, inner, turn


def peer(loop, grp, i):
    k = lax.rem(i * STRIDE, DEV)
    z = lax.rem(lax.div(loop, 2) + lax.div(k, 16), 4)
    c = lax.rem(loop + lax.div(k, 64), 2)
    y = lax.rem(lax.div(grp, 4) + lax.div(k, 4), 4)
    x = lax.rem(grp + k, 4)
    return z * 2 + c, y * 4 + x


def times(a, b):
    return a[0] * b[0] - a[1] * b[1], a[0] * b[1] + a[1] * b[0]


def times_conj(a, b):
    return a[0] * b[0] + a[1] * b[1], a[1] * b[0] - a[0] * b[1]


def four(a, b, c, d, forward):
    s0, s1 = (a[0] + c[0], a[1] + c[1]), (a[0] - c[0], a[1] - c[1])
    s2, s3 = (b[0] + d[0], b[1] + d[1]), (b[0] - d[0], b[1] - d[1])
    s3 = (s3[1], -s3[0]) if forward else (-s3[1], s3[0])
    return (
        (s0[0] + s2[0], s0[1] + s2[1]),
        (s1[0] + s3[0], s1[1] + s3[1]),
        (s0[0] - s2[0], s0[1] - s2[1]),
        (s1[0] - s3[0], s1[1] - s3[1]),
    )


def sixteen(values, forward):
    sign = -1.0 if forward else 1.0
    parts = []
    for low in range(4):
        out = four(*[values[4 * high + low] for high in range(4)], forward)
        turned = []
        for k, v in enumerate(out):
            m = low * k
            if m == 0:
                turned.append(v)
            elif m == 4:
                turned.append((-sign * v[1], sign * v[0]))
            else:
                angle = sign * 2.0 * math.pi * m / 16
                turned.append(times(v, (math.cos(angle), math.sin(angle))))
        parts.append(turned)
    result = [None] * 16
    for k in range(4):
        out = four(*[parts[low][k] for low in range(4)], forward)
        for high in range(4):
            result[k + 4 * high] = out[high]
    return result


def kernel(
    tokens, taps_hbm, columns_hbm, across_hbm, inner_hbm, turn_hbm, mixed,
    first, send_two, second, middle, send_three, third, send_four, total,
    out_high, out_low, back_high, back_low, taps, columns, across, inner, turn,
    send_sem, recv_sem, local_sem,
):
    loop = lax.axis_index("loop")
    grp = lax.axis_index("grp")
    me = loop * 16 + grp
    bar = pltpu.get_barrier_semaphore()

    def rows(start, size):
        return pl.ds(pl.multiple_of(start, 8), size)

    loads = [
        pltpu.make_async_copy(src, dst, local_sem.at[n])
        for n, (src, dst) in enumerate(
            ((columns_hbm, columns), (across_hbm, across), (inner_hbm, inner), (turn_hbm, turn), (taps_hbm, taps.at[rows(0, 8192)]))
        )
    ]
    for load in loads[:2]:
        load.start()

    groups = [lax.rem(grp + n, 16) for n in range(16)]

    def greet(i, _):
        other = lax.rem(loop + i, 8)
        for group in groups:
            pl.semaphore_signal(bar, inc=1, device_id=(other, group), device_id_type=MESH)
        return 0

    for group in groups[1:]:
        pl.semaphore_signal(bar, inc=1, device_id=(loop, group), device_id_type=MESH)
    lax.fori_loop(1, 8, greet, 0)
    pl.semaphore_wait(bar, DEV - 1)

    def scatter(n, src, dst, size, src_at, dst_at):
        own = pltpu.make_async_copy(src.at[rows(src_at(me), size)], dst.at[rows(dst_at(me), size)], local_sem.at[5 + n])
        own.start()

        def send(i):
            l, g = peer(loop, grp, i)
            pltpu.make_async_remote_copy(
                src.at[rows(src_at(l * 16 + g), size)],
                dst.at[rows(dst_at(me), size)],
                send_sem.at[n],
                recv_sem.at[n],
                device_id=(l, g),
                device_id_type=MESH,
            ).start()

        def send_three(t, _):
            for u in range(3):
                send(2 + 3 * t + u)
            return 0

        send(1)
        lax.fori_loop(0, (DEV - 2) // 3, send_three, 0)
        count = (DEV - 1) * size
        whole = pltpu.make_async_remote_copy(
            src.at[rows(0, count)],
            dst.at[rows(0, count)],
            send_sem.at[n],
            recv_sem.at[n],
            device_id=(loop, grp),
            device_id_type=MESH,
        )
        return whole, own

    def arrive(move):
        move[0].wait_recv()
        move[1].wait()

    def block(e, h, halves):
        if halves:
            return e * 4096 + h * 2048, 16
        return e * 4096 + h * 16, 32

    def strided(e, r, c, halves):
        base, stride = block(e, r // 8, halves)
        return pl.ds(base + c * 8 + r % 8, DEV, stride=stride)

    def exchange(n, src, dst, e, h, halves):
        base, stride = block(e, h, halves)
        at = lambda d: base + d * stride
        return scatter(n, src, dst, stride, at, at)

    move_one = [
        scatter(h, tokens, first, 8, lambda d: d * ROWS + h * 8, lambda d: h * 1024 + d * 8) for h in range(2)
    ]

    for load in loads[2:]:
        load.start()
    loads[0].wait()
    loads[1].wait()
    lane = lax.broadcasted_iota(jnp.int32, (16, LANES), 1)

    def build_out(t, _):
        at = pl.multiple_of(t * 16, 16)
        e, p = t // 8, pl.multiple_of((t % 8) * 16, 16)
        part = [columns[pl.ds(n * 256 + at, 16), :] for n in range(6)]
        shift = [jnp.sum(jnp.where(lane == me, v, 0.0), axis=1, keepdims=True) for v in part[2:4]]
        value = times(part[0:2], shift)
        for r in range(ROWS):
            for c in range(2):
                high, low = split(value[c])
                dst = pl.ds(((r * 2 + e) * 2 + c) * DEV + p, 16)
                out_high[dst, :] = high
                out_low[dst, :] = low
            if r < ROWS - 1:
                value = times(value, part[4:6])
        return 0

    lax.fori_loop(0, 16, build_out, 0)

    def build_back(t, _):
        at = pl.multiple_of(t * 16, 16)
        base = [across[pl.ds(n * DEV + at, 16), :] for n in range(2)]
        shift = [across[pl.ds((2 + n) * DEV + me, 1), :] for n in range(2)]
        step = [across[pl.ds(4 * DEV + n * 8, 1), :] for n in range(2)]
        value = times(base, shift)
        for r in range(ROWS):
            for c in range(2):
                high, low = split(value[c])
                for e in range(2):
                    dst = pl.ds((r * 2 + e) * DEV + at, 16)
                    back_high[dst, c * DEV : (c + 1) * DEV] = high[:, e * DEV : (e + 1) * DEV]
                    back_low[dst, c * DEV : (c + 1) * DEV] = low[:, e * DEV : (e + 1) * DEV]
            if r < ROWS - 1:
                value = times(value, step)
        return 0

    lax.fori_loop(0, 8, build_back, 0)

    def analyse(e, h):
        for r in range(8 * h, 8 * h + 8):
            at = (r * 2 + e) * 256
            value = dot_four(
                out_high[at : at + 256, :],
                out_low[at : at + 256, :],
                first[pl.ds(h * 1024 + r % 8, DEV, stride=8), :],
            )
            for c in range(2):
                send_two[strided(e, r, c, e == 0), :] = value[c * DEV : (c + 1) * DEV]

    arrive(move_one[0])
    analyse(0, 0)
    move_two = [exchange(2, send_two, second, 0, 0, True)]
    analyse(1, 0)
    arrive(move_one[1])
    analyse(0, 1)
    move_two.append(exchange(3, send_two, second, 0, 1, True))
    analyse(1, 1)
    move_two.append(exchange(4, send_two, second, 1, 0, False))

    for load in loads[2:]:
        load.wait()

    move_three = []
    for e in range(2):
        for move in move_two[2 * e : 2 * e + 2]:
            arrive(move)
        for b in range(0, ROWS, 2):
            value = jnp.concatenate(
                [
                    jnp.concatenate(
                        [second[strided(e, b + n, c, e == 0), :] for c in range(2)], axis=0
                    )
                    for n in range(2)
                ],
                axis=1,
            )
            value = dot_three(inner[0:256, :], inner[512:768, :], value)
            for n in range(2):
                middle[(b + n) * 256 : (b + n + 1) * 256, :] = value[:, n * LANES : (n + 1) * LANES]

        def filtered(t, _):
            at = pl.multiple_of(t * 8, 8)
            turns = [[turn[pl.ds(c * 2048 + b * DEV + at, 8), :] for c in range(2)] for b in range(ROWS)]
            value = [[middle[pl.ds(b * 256 + c * DEV + at, 8), :] for c in range(2)] for b in range(ROWS)]
            value = [value[0]] + [times(value[b], turns[b]) for b in range(1, ROWS)]
            value = sixteen(value, True)
            value = [
                times(value[q], [taps[pl.ds(c * 4096 + q * 256 + e + 2 * at, 8, stride=2), :] for c in range(2)])
                for q in range(ROWS)
            ]
            value = sixteen(value, False)
            value = [value[0]] + [times_conj(value[b], turns[b]) for b in range(1, ROWS)]
            for b in range(ROWS):
                for c in range(2):
                    middle[pl.ds(b * 256 + c * DEV + at, 8), :] = value[b][c]
            return 0

        lax.fori_loop(0, DEV // 8, filtered, 0)
        for b in range(0, ROWS, 2):
            value = jnp.concatenate([middle[(b + n) * 256 : (b + n + 1) * 256, :] for n in range(2)], axis=1)
            value = dot_three(inner[256:512, :], inner[768:1024, :], value)
            for n in range(2):
                for c in range(2):
                    send_three[strided(e, b + n, c, e == 1), :] = value[
                        c * DEV : (c + 1) * DEV, n * LANES : (n + 1) * LANES
                    ]
            if e == 1 and b == 6:
                move_three.append(exchange(6, send_three, third, 1, 0, True))
        move_three.append(exchange(5 + 2 * e, send_three, third, e, e, e == 1))

    def combine(e, r):
        at = (r * 2 + e) * DEV
        value = jnp.concatenate([third[strided(e, r, c, e == 1), :] for c in range(2)], axis=0)
        return dot_four(back_high[at : at + DEV, :], back_low[at : at + DEV, :], value)

    arrive(move_three[0])
    for r in range(ROWS):
        total[r * DEV : (r + 1) * DEV, :] = combine(0, r)
    move_four = []
    for h in range(2):
        arrive(move_three[1 + h])
        for r in range(8 * h, 8 * h + 8):
            send_four[pl.ds(h * 1024 + r % 8, DEV, stride=8), :] = total[r * DEV : (r + 1) * DEV, :] + combine(1, r)
        move_four.append(
            scatter(8 + h, send_four, mixed, 8, lambda d: h * 1024 + d * 8, lambda d: d * ROWS + h * 8)
        )
    for move in move_four:
        arrive(move)
    for move in (*move_one, *move_two, *move_three, *move_four):
        move[0].wait_send()


def body(tokens, filter_spec, skip_gain):
    columns, across, inner, turn = tables()
    hbm = pl.BlockSpec(memory_space=pl.ANY)
    f32, bf16 = jnp.float32, jnp.bfloat16
    result = pl.pallas_call(
        kernel,
        out_shape=jax.ShapeDtypeStruct((2048, LANES), f32),
        in_specs=[hbm] * 6,
        out_specs=hbm,
        scratch_shapes=[
            pltpu.VMEM((2048 + PAD, LANES), f32),
            pltpu.VMEM((8192 + PAD, LANES), f32),
            pltpu.VMEM((8192 + PAD, LANES), f32),
            pltpu.VMEM((4096, LANES), f32),
            pltpu.VMEM((8192 + PAD, LANES), f32),
            pltpu.VMEM((8192 + PAD, LANES), f32),
            pltpu.VMEM((2048 + PAD, LANES), f32),
            pltpu.VMEM((2048 + PAD, LANES), f32),
            pltpu.VMEM((8192, LANES), bf16),
            pltpu.VMEM((8192, LANES), bf16),
            pltpu.VMEM((4096, 256), bf16),
            pltpu.VMEM((4096, 256), bf16),
            pltpu.VMEM((8192 + PAD, LANES), f32),
            pltpu.VMEM(columns.shape, f32),
            pltpu.VMEM(across.shape, f32),
            pltpu.VMEM(inner.shape, bf16),
            pltpu.VMEM(turn.shape, f32),
            pltpu.SemaphoreType.DMA((10,)),
            pltpu.SemaphoreType.DMA((10,)),
            pltpu.SemaphoreType.DMA((15,)),
        ],
        compiler_params=pltpu.CompilerParams(
            collective_id=0, has_side_effects=True, vmem_limit_bytes=56 * 2**20
        ),
    )(
        tokens,
        filter_spec.reshape(8192, LANES),
        jnp.asarray(columns),
        jnp.asarray(across),
        jnp.asarray(inner),
        jnp.asarray(turn),
    )
    return result * (1.0 / FULL) + skip_gain[None, :] * tokens


def solution(mesh):
    in_specs = (P(("loop", "grp"), None), P(None, None, ("loop", "grp"), None, None), P())
    out_specs = P(("loop", "grp"), None)
    return jax.shard_map(body, mesh=mesh, in_specs=in_specs, out_specs=out_specs, check_vma=False)
```
